256 devices in a mesh: depth: 8 (over y, core), row: 8 (over x, z_lo), col: 4 (over z_hi).
Axes of the slice: x: 4, y: 4, z: 8 (z_hi: 4, z_lo: 2; z = z_hi * 2 + z_lo), core: 2. Of those that a mesh axis runs over, the one named last changes fastest.
Arguments:
- acts: bfloat16 [5120, 6144], P(('depth', 'col'), 'row'), may hold values from -6 to 6
- w_out: bfloat16 [6144, 12288], P(('depth', 'col'), 'row'), may hold values from -0.078125 to 0.078125
- grad_out: bfloat16 [5120, 12288], P(('depth', 'col'), 'row'), may hold values from -6 to 6
Outputs:
- outputs: bfloat16 [5120, 12288], P(('depth', 'col'), 'row')
- grad_acts: bfloat16 [5120, 6144], P(('depth', 'col'), 'row')
- w_grad: bfloat16 [6144, 12288], P(('depth', 'col'), 'row')
The draws below stay inside these ranges and needn't reach their ends.
All inputs are finite; a program needn't handle non-finite values.
Results may differ from the reference program's by a relative error of at most 0.019.
Values may be sent and summed in bfloat16 or wider, within the bound.
A program may use at most 128 MiB of HBM per device.

```python
import jax
import jax.numpy as jnp
from jax import lax

D = 12288
TOK_DEV = 160
K = 6144
TOKENS = 5120
N_DEPTH = 8
N_COL = 4


def with_spikes(drawn, own_key, source, target, blocks, factor):
    def block_of(dim):
        return (jnp.arange(drawn.shape[dim]) // (drawn.shape[dim] // blocks)).reshape((-1,) + (1,) * (drawn.ndim - 1 - dim))

    near = jax.random.permutation(own_key, blocks)[block_of(target)]
    second = (block_of(target) + blocks // 2) % blocks
    return jnp.where((block_of(source) == near) | (block_of(source) == second), factor * drawn, drawn)


def block_levels(own_key, shape, pieces, low, top_value):
    gain = 1.0
    for position, parts in pieces:
        draws = jax.random.uniform(jax.random.fold_in(jax.random.fold_in(own_key, 6), position), (parts,), jnp.float32, low / len(pieces), top_value / len(pieces))
        gain = gain * jnp.repeat(jnp.exp(draws), shape[position] // parts).reshape((-1,) + (1,) * (len(shape) - 1 - position))
    return gain


def noise(own_key, dims, scale, reach, shards=(), held_as=jnp.bfloat16):
    values = jax.random.normal(own_key, dims, jnp.float32) * scale
    if len(shards) > 0:
        values = block_levels(own_key, dims, shards, -0.22, 0.18) * values
    return jnp.clip(values, min=-reach, max=reach).astype(held_as)


def noise_with(rng, dims, width, limit, split, heavy, dtype=jnp.bfloat16):
    values = width * jax.random.normal(rng, dims, jnp.float32)
    if split:
        values = values * block_levels(rng, dims, split, -0.22, 0.18)
    return jnp.clip(with_spikes(values, jax.random.fold_in(rng, 3), *heavy), -limit, limit).astype(dtype)


def setup_inputs(seed: int = 0) -> dict:
    streams_of = jax.random.split(jax.random.key(seed), 4)
    return {
        "acts": noise_with(streams_of[0], (TOKENS, K), 1.0, 6.0, ((0, 32), (1, 8)), (0, 1, 32, 2.75)),
        "w_out": noise(streams_of[1], (K, D), K ** -0.5, 0.078125, ((0, 32), (1, 8))),
        "grad_out": noise(streams_of[2], (TOKENS, D), 1.0, 6.0, ((0, 32), (1, 8))),
    }


def reference(acts, w_out, grad_out):
    outputs = jnp.dot(acts, w_out, preferred_element_type=jnp.float32).astype(jnp.bfloat16)
    grad_acts = jnp.dot(grad_out, w_out.T, preferred_element_type=jnp.float32).astype(jnp.bfloat16)
    act_groups = acts.reshape(N_DEPTH, TOK_DEV * N_COL, K)
    grad_groups = grad_out.reshape(N_DEPTH, TOK_DEV * N_COL, D)

    def add_group(total, pair):
        act_part, grad_part = pair
        part = jnp.dot(act_part.T, grad_part, preferred_element_type=jnp.float32).astype(jnp.bfloat16)
        part = lax.optimization_barrier(part)
        return total + part.astype(jnp.float32), None

    total, _ = lax.scan(add_group, jnp.zeros((K, D), jnp.float32), (act_groups, grad_groups))
    return outputs, grad_acts, total.astype(jnp.bfloat16)
```

```python
import jax
import jax.numpy as jnp
from jax import lax
from jax.sharding import PartitionSpec as P


def per_device(acts, w_out, grad_out):
    rows, feats = acts.shape
    cols = lax.axis_size("col")
    piece = feats // cols
    parted = lax.all_to_all(
        acts.reshape(rows, cols, piece), "col", split_axis=1, concat_axis=0, tiled=True
    )
    a = lax.all_gather(parted.reshape(rows * cols, piece), "row", axis=1, tiled=True)
    w = lax.all_gather(w_out, "depth", axis=0, tiled=True)
    g = lax.all_gather(grad_out, "col", axis=0, tiled=True)
    y = jnp.dot(a, w, preferred_element_type=jnp.float32).astype(jnp.bfloat16)
    outputs = lax.psum_scatter(y, "col", scatter_dimension=0, tiled=True)
    ga = lax.dot_general(
        g, w, (((1,), (1,)), ((), ())), preferred_element_type=jnp.float32
    ).astype(jnp.bfloat16)
    ga = lax.psum_scatter(ga, "row", scatter_dimension=1, tiled=True)
    ga = lax.all_to_all(
        ga.reshape(cols, rows, piece), "col", split_axis=0, concat_axis=0, tiled=True
    )
    grad_acts = ga.transpose(1, 0, 2).reshape(rows, feats)
    gw = lax.dot_general(
        a, g, (((0,), (0,)), ((), ())), preferred_element_type=jnp.float32
    ).astype(jnp.bfloat16)
    w_grad = lax.psum_scatter(gw, "depth", scatter_dimension=0, tiled=True)
    return (outputs, grad_acts, w_grad)


def solution(mesh):
    spec = P(("depth", "col"), "row")
    return jax.shard_map(
        per_device, mesh=mesh, in_specs=(spec,) * 3, out_specs=(spec,) * 3, check_vma=False
    )
```

```python
import jax
import jax.numpy as jnp
from jax import lax
from jax.experimental import pallas as pl
from jax.experimental.pallas import tpu as pltpu
from jax.sharding import PartitionSpec as P

MESH = pl.DeviceIdType.MESH
BF = jnp.bfloat16
F32 = jnp.float32

M1 = 160
MG = 640
KB = 192
XB = 384
N = 1536
H = 80
NC = 512
NJ = N // NC

S_AM, S_AR, S_AX, S_WY, S_WC, S_G, S_Y, S_GX, S_GM, S_GR, S_CS, S_WS = (
    0, 8, 16, 19, 22, 26, 32, 50, 53, 61, 69, 73,
)
N_SEM = 76


def kernel(
    am_in, ar_in, w_in, g_in,
    y_out, gm_out, gr_out, w_out,
    a4, arb, wb, gb, at4, yp, ysend, yrecv, gs, grecv, sx, srem, fm, fr,
    gw, cs, crecv, ws, wrecv, ss, rs, ls,
):
    d, r, c = lax.axis_index("depth"), lax.axis_index("row"), lax.axis_index("col")
    y, k = d // 2, lax.rem(d, 2)
    x, l = r // 2, lax.rem(r, 2)

    def xdev(i):
        return (d, 2 * lax.rem(x + i, 4) + l, c)

    def ydev(i):
        return (2 * lax.rem(y + i, 4) + k, r, c)

    def zdev(dc, dl):
        return (d, 2 * x + lax.rem(l + dl, 2), lax.rem(c + dc, 4))

    sib = (2 * y + 1 - k, r, c)
    offs = [(dc, dl) for dc in (2, 1, 3, 0) for dl in (0, 1) if (dc, dl) != (0, 0)]

    bar = pltpu.get_barrier_semaphore()
    peers = [zdev(*o) for o in offs] + [xdev(i) for i in (1, 2, 3)]
    peers += [ydev(i) for i in (1, 2, 3)] + [sib]
    for p in peers:
        pl.semaphore_signal(bar, inc=1, device_id=p, device_id_type=MESH)
    pl.semaphore_wait(bar, len(peers))

    pending = []

    def copy(src, dst, sem, dev):
        return pltpu.make_async_remote_copy(
            src, dst, ss.at[sem], rs.at[sem], device_id=dev, device_id_type=MESH
        )

    def send(src, dst, sem, dev):
        cp = copy(src, dst, sem, dev)
        cp.start()
        pending.append(cp)

    def arrived(dst, sem, dev):
        copy(dst, dst, sem, dev).wait_recv()

    def rows(i, size):
        return pl.ds(pl.multiple_of(i * size, 16), size)

    def main_lane(q):
        return pl.ds(pl.multiple_of(q * 256, 128), 128)

    for dc, dl in offs:
        t = lax.rem(c + dc, 4)
        o = 2 * dc + dl
        send(am_in.at[t], a4.at[x, rows(c, M1), main_lane(l)], S_AM + o, zdev(dc, dl))
        send(ar_in.at[t], arb.at[2 * c + l], S_AR + o, zdev(dc, dl))
    h0, h1 = pl.ds(0, H), pl.ds(H, H)

    def grow(block, half):
        return pl.ds(pl.multiple_of(block * M1 + half * H, 16), H)

    send(g_in.at[h0], gb.at[grow(c, 0)], S_G + 0, zdev(1, 0))
    send(g_in.at[h1], gb.at[grow(c, 1)], S_G + 1, zdev(3, 0))
    for i in (2, 1, 3):
        send(w_in, wb.at[rows(d, KB)], S_WY + i - 1, ydev(i))
    send(w_in, wb.at[rows(d, KB)], S_WC + 0, sib)
    send(g_in.at[h1], gb.at[grow(c, 1)], S_G + 2, zdev(1, 0))
    send(g_in.at[h0], gb.at[grow(c, 0)], S_G + 3, zdev(3, 0))

    own = [
        pltpu.make_async_copy(am_in.at[c], a4.at[x, rows(c, M1), main_lane(l)], ls.at[0]),
        pltpu.make_async_copy(ar_in.at[c], arb.at[2 * c + l], ls.at[1]),
        pltpu.make_async_copy(w_in, wb.at[rows(d, KB)], ls.at[2]),
        pltpu.make_async_copy(g_in, gb.at[rows(c, M1)], ls.at[3]),
    ]
    for cp in own:
        cp.start()
    own[0].wait()
    own[1].wait()

    for dc, dl in offs:
        cc, ll = lax.rem(c + 4 - dc, 4), lax.rem(l + dl, 2)
        o = 2 * dc + dl
        arrived(a4.at[x, rows(cc, M1), main_lane(ll)], S_AM + o, zdev(dc, dl))
        arrived(arb.at[2 * cc + ll], S_AR + o, zdev(dc, dl))
    lane = lax.broadcasted_iota(jnp.int32, (H, 128), 1)
    left = lane < 64
    for q in range(4):
        p0, p1 = arb[2 * q].astype(F32), arb[2 * q + 1].astype(F32)
        low = jnp.where(left, p0, p1)
        high = pltpu.roll(jnp.where(left, p1, p0), 64, 1)
        a4[x, pl.ds(q * M1, H), pl.ds(128, 128)] = low.astype(BF)
        a4[x, pl.ds(q * M1 + H, H), pl.ds(128, 128)] = high.astype(BF)
    for i in (2, 1, 3):
        send(a4.at[x], a4.at[x], S_AX + i - 1, xdev(i))

    cl, cr, co = lax.rem(c + 3, 4), lax.rem(c + 1, 4), lax.rem(c + 2, 4)
    arrived(gb.at[grow(cl, 0)], S_G + 0, zdev(1, 0))
    send(gb.at[grow(cl, 0)], gb.at[grow(cl, 0)], S_G + 4, zdev(1, 0))
    arrived(gb.at[grow(cr, 1)], S_G + 1, zdev(3, 0))
    send(gb.at[grow(cr, 1)], gb.at[grow(cr, 1)], S_G + 5, zdev(3, 0))

    own[2].wait()
    own[3].wait()
    for i in (1, 3, 2):
        src = 2 * lax.rem(y + 4 - i, 4) + k
        arrived(wb.at[rows(src, KB)], S_WY + i - 1, ydev(i))
        send(wb.at[rows(src, KB)], wb.at[rows(src, KB)], S_WC + i, sib)

    for i in (1, 3, 2):
        src = lax.rem(x + 4 - i, 4)
        arrived(a4.at[src], S_AX + i - 1, xdev(i))
    for i in (0, 1, 3, 2):
        src = 2 * lax.rem(y + 4 - i, 4) + 1 - k
        arrived(wb.at[rows(src, KB)], S_WC + i, sib)

    def yrow(block, half):
        return pl.ds(pl.multiple_of(block * M1 + half * H, 16), H)

    for j in range(NJ):
        @pl.loop(0, NC // 256)
        def _(t):
            cols = pl.ds(pl.multiple_of(j * NC + t * 256, 256), 256)
            a = jnp.concatenate([a4[0], a4[1], a4[2], a4[3]], axis=1)
            yp[:, cols] = jnp.dot(a, wb[:, cols], preferred_element_type=F32)

        cols = pl.ds(j * NC, NC)
        for kind, block, half, dc in ((0, co, 0, 1), (1, co, 1, 3), (2, cr, 1, 1), (3, cl, 0, 3)):
            ysend[kind, j] = yp[yrow(block, half), cols].astype(BF)
            send(ysend.at[kind, j], yrecv.at[kind, j], S_Y + 3 * kind + j, zdev(dc, 0))

    for q in range(4):
        at4[q] = a4[q].T

    arrived(gb.at[grow(cl, 1)], S_G + 2, zdev(1, 0))
    arrived(gb.at[grow(cr, 0)], S_G + 3, zdev(3, 0))
    arrived(gb.at[grow(co, 0)], S_G + 4, zdev(1, 0))
    arrived(gb.at[grow(co, 1)], S_G + 5, zdev(3, 0))

    def nt_dot(a, b):
        return lax.dot_general(a, b, (((1,), (1,)), ((), ())), preferred_element_type=F32)

    for pair in ((2, 1), (3, 0)):
        xa, xb = lax.rem(x + pair[0], 4), lax.rem(x + pair[1], 4)
        wa = pl.multiple_of(xa * XB, 128)
        wc = pl.multiple_of(xb * XB, 128)
        g = gb[...]
        gs[pair[0], :, 0:256] = nt_dot(g, wb[pl.ds(wa, 256), :]).astype(BF)
        mid = jnp.concatenate([wb[pl.ds(wa + 256, 128), :], wb[pl.ds(wc, 128), :]], axis=0)
        mid = nt_dot(g, mid).astype(BF)
        gs[pair[0], :, 256:384] = mid[:, :128]
        gs[pair[1], :, 0:128] = mid[:, 128:]
        gs[pair[1], :, 128:384] = nt_dot(g, wb[pl.ds(wc + 128, 256), :]).astype(BF)
        for i in pair:
            if i:
                send(gs.at[i], grecv.at[i - 1], S_GX + i - 1, xdev(i))

    def relay():
        for j in range(NJ):
            cols = pl.ds(j * NC, NC)
            arrived(yrecv.at[0, j], S_Y + j, zdev(1, 0))
            ysend[4, j] = (yp[yrow(cr, 0), cols] + yrecv[0, j].astype(F32)).astype(BF)
            send(ysend.at[4, j], yrecv.at[4, j], S_Y + 12 + j, zdev(1, 0))
            arrived(yrecv.at[1, j], S_Y + 3 + j, zdev(3, 0))
            ysend[5, j] = (yp[yrow(cl, 1), cols] + yrecv[1, j].astype(F32)).astype(BF)
            send(ysend.at[5, j], yrecv.at[5, j], S_Y + 15 + j, zdev(3, 0))

    relay()

    for pair in ((2, 1), (3, 0)):
        ya, yb = lax.rem(y + pair[0], 4), lax.rem(y + pair[1], 4)

        @pl.loop(0, N // 256)
        def _(t):
            cols = pl.ds(pl.multiple_of(t * 256, 256), 256)
            at = jnp.concatenate([at4[ya], at4[yb]], axis=0)
            acc = jnp.dot(at, gb[:, cols], preferred_element_type=F32)
            for q in range(4):
                gw[2 * pair[q // 2] + q % 2, :, cols] = acc[q * KB : (q + 1) * KB]

        for i in pair:
            cs[i] = gw[2 * i + 1 - k].astype(BF)
            send(cs.at[i], crecv.at[i], S_CS + i, sib)

    for i in (2, 1, 3):
        arrived(crecv.at[i], S_CS + i, sib)
        ws[i - 1] = (gw[2 * i + k] + crecv[i].astype(F32)).astype(BF)
        send(ws.at[i - 1], wrecv.at[i - 1], S_WS + i - 1, ydev(i))
    arrived(crecv.at[0], S_CS + 0, sib)

    for i in (1, 3, 2):
        arrived(grecv.at[i - 1], S_GX + i - 1, xdev(i))
    total = gs[0].astype(F32) + grecv[0].astype(F32)
    total += grecv[1].astype(F32) + grecv[2].astype(F32)
    sx[...] = total.astype(BF)
    for q in range(4):
        t0 = sx[pl.ds(q * M1, H), pl.ds(128, 128)].astype(F32)
        t1 = pltpu.roll(sx[pl.ds(q * M1 + H, H), pl.ds(128, 128)].astype(F32), 64, 1)
        srem[2 * q] = jnp.where(left, t0, t1).astype(BF)
        srem[2 * q + 1] = jnp.where(left, t1, t0).astype(BF)
    for dc, dl in offs:
        cc, ll = lax.rem(c + dc, 4), lax.rem(l + dl, 2)
        o = 2 * dc + dl
        send(sx.at[rows(cc, M1), main_lane(ll)], fm.at[2 * c + l], S_GM + o, zdev(dc, dl))
        send(srem.at[2 * cc + ll], fr.at[2 * c + l], S_GR + o, zdev(dc, dl))
    fm[2 * c + l] = sx[rows(c, M1), main_lane(l)]
    fr[2 * c + l] = srem[2 * c + l]

    for j in range(NJ):
        cols = pl.ds(j * NC, NC)
        for kind, dc in ((2, 1), (3, 3), (4, 1), (5, 3)):
            arrived(yrecv.at[kind, j], S_Y + 3 * kind + j, zdev(dc, 0))
        y_out[h0, cols] = (
            yp[yrow(c, 0), cols] + yrecv[4, j].astype(F32) + yrecv[3, j].astype(F32)
        ).astype(BF)
        y_out[h1, cols] = (
            yp[yrow(c, 1), cols] + yrecv[5, j].astype(F32) + yrecv[2, j].astype(F32)
        ).astype(BF)

    for i in (1, 3, 2):
        arrived(wrecv.at[i - 1], S_WS + i - 1, ydev(i))
    w_out[...] = (
        gw[k] + crecv[0].astype(F32)
        + wrecv[0].astype(F32) + wrecv[1].astype(F32) + wrecv[2].astype(F32)
    ).astype(BF)

    for dc, dl in offs:
        cc, ll = lax.rem(c + 4 - dc, 4), lax.rem(l + dl, 2)
        o = 2 * dc + dl
        arrived(fm.at[2 * cc + ll], S_GM + o, zdev(dc, dl))
        arrived(fr.at[2 * cc + ll], S_GR + o, zdev(dc, dl))
    for q in range(4):
        gm_out[q] = (fm[2 * q].astype(F32) + fm[2 * q + 1].astype(F32)).astype(BF)
        gr_out[q] = (fr[2 * q].astype(F32) + fr[2 * q + 1].astype(F32)).astype(BF)

    for cp in pending:
        cp.wait_send()


def per_device(acts, w_out, grad_out):
    odd = lax.rem(lax.axis_index("row"), 2) == 1
    a3 = acts.reshape(M1, 4, KB).transpose(1, 0, 2)
    main = jnp.where(odd, a3[:, :, 64:], a3[:, :, :128])
    rem = jnp.where(odd, a3[:, :, :64], a3[:, :, 128:])
    top, low = rem[:, :H], rem[:, H:]
    rem = jnp.where(
        odd, jnp.concatenate([low, top], axis=-1), jnp.concatenate([top, low], axis=-1)
    )

    def vm(shape, dtype=BF):
        return pltpu.VMEM(shape, dtype)

    outputs, gm, gr, w_grad = pl.pallas_call(
        kernel,
        out_shape=[
            jax.ShapeDtypeStruct((M1, N), BF),
            jax.ShapeDtypeStruct((4, M1, 128), BF),
            jax.ShapeDtypeStruct((4, H, 128), BF),
            jax.ShapeDtypeStruct((KB, N), BF),
        ],
        in_specs=[pl.BlockSpec(memory_space=pltpu.VMEM)] * 4,
        out_specs=[pl.BlockSpec(memory_space=pltpu.VMEM)] * 4,
        scratch_shapes=[
            vm((4, MG, XB)),
            vm((8, H, 128)),
            vm((N, N)),
            vm((MG, N)),
            vm((4, XB, MG)),
            vm((MG, N), F32),
            vm((6, NJ, H, NC)),
            vm((6, NJ, H, NC)),
            vm((4, MG, XB)),
            vm((3, MG, XB)),
            vm((MG, XB)),
            vm((8, H, 128)),
            vm((8, M1, 128)),
            vm((8, H, 128)),
            vm((8, KB, N), F32),
            vm((4, KB, N)),
            vm((4, KB, N)),
            vm((3, KB, N)),
            vm((3, KB, N)),
            pltpu.SemaphoreType.DMA((N_SEM,)),
            pltpu.SemaphoreType.DMA((N_SEM,)),
            pltpu.SemaphoreType.DMA((4,)),
        ],
        compiler_params=pltpu.CompilerParams(
            collective_id=0, has_side_effects=True, vmem_limit_bytes=60 * 2**20
        ),
        cost_estimate=pl.CostEstimate(
            flops=6 * MG * N * N, bytes_accessed=3 * 2**20, transcendentals=0
        ),
    )(main, rem, w_out, grad_out)

    a, b = gr[:, :, :64], gr[:, :, 64:]
    rem = jnp.where(odd, jnp.concatenate([b, a], axis=1), jnp.concatenate([a, b], axis=1))
    a3 = jnp.where(
        odd, jnp.concatenate([rem, gm], axis=-1), jnp.concatenate([gm, rem], axis=-1)
    )
    grad_acts = a3.transpose(1, 0, 2).reshape(M1, 4 * KB)
    return outputs, grad_acts, w_grad


def solution(mesh):
    spec = P(("depth", "col"), "row")
    return jax.shard_map(
        per_device, mesh=mesh, in_specs=(spec,) * 3, out_specs=(spec,) * 3, check_vma=False
    )
```

```python
import jax
import jax.numpy as jnp
from jax import lax
from jax.experimental import pallas as pl
from jax.experimental.pallas import tpu as pltpu
from jax.sharding import PartitionSpec as P

MESH = pl.DeviceIdType.MESH
BF = jnp.bfloat16
F32 = jnp.float32

M1 = 160
MG = 640
KB = 192
XB = 384
N = 1536
H = 80
NC = 512
NJ = N // NC

S_AM, S_AR, S_AX, S_WY, S_WC, S_G, S_Y, S_GX, S_GM, S_GR, S_CS, S_WS = (
    0, 8, 16, 19, 22, 26, 32, 50, 53, 61, 69, 73,
)
N_SEM = 76


def kernel(
    acts, w_in, g_in,
    y_out, ga_out, w_out,
    am_in, ar_in, a4, arb, wb, gb, at4, yp, ysend, yrecv, gs, grecv, sx, srem, fm, fr,
    gw, cs, crecv, ws, wrecv, ss, rs, ls,
):
    d, r, c = lax.axis_index("depth"), lax.axis_index("row"), lax.axis_index("col")
    y, k = d // 2, lax.rem(d, 2)
    x, l = r // 2, lax.rem(r, 2)

    def xdev(i):
        return (d, 2 * lax.rem(x + i, 4) + l, c)

    def ydev(i):
        return (2 * lax.rem(y + i, 4) + k, r, c)

    def zdev(dc, dl):
        return (d, 2 * x + lax.rem(l + dl, 2), lax.rem(c + dc, 4))

    sib = (2 * y + 1 - k, r, c)
    offs = [(dc, dl) for dc in (2, 1, 3, 0) for dl in (0, 1) if (dc, dl) != (0, 0)]

    bar = pltpu.get_barrier_semaphore()
    peers = [zdev(*o) for o in offs] + [xdev(i) for i in (1, 2, 3)]
    peers += [ydev(i) for i in (1, 2, 3)] + [sib]
    for p in peers:
        pl.semaphore_signal(bar, inc=1, device_id=p, device_id_type=MESH)
    pl.semaphore_wait(bar, len(peers))

    pending = []

    def copy(src, dst, sem, dev):
        return pltpu.make_async_remote_copy(
            src, dst, ss.at[sem], rs.at[sem], device_id=dev, device_id_type=MESH
        )

    def send(src, dst, sem, dev):
        cp = copy(src, dst, sem, dev)
        cp.start()
        pending.append(cp)

    def arrived(dst, sem, dev):
        copy(dst, dst, sem, dev).wait_recv()

    def rows(i, size):
        return pl.ds(pl.multiple_of(i * size, 16), size)

    def main_lane(q):
        return pl.ds(pl.multiple_of(q * 256, 128), 128)

    lane = lax.broadcasted_iota(jnp.int32, (M1, 128), 1)
    left = lane < 64
    left_h = left[:H]

    def swap(v):
        return pltpu.roll(v, 64, 1)

    def pack(lv):
        def tile(q):
            return acts[:, 128 * q : 128 * q + 128].astype(F32)

        for t in range(4):
            q, odd = divmod(KB * t + 64 * lv, 128)
            if odd:
                am_in[t] = swap(jnp.where(left, tile(q + 1), tile(q))).astype(BF)
            else:
                am_in[t] = acts[:, 128 * q : 128 * q + 128]
            q, odd = divmod(KB * t + 128 * (1 - lv), 128)
            first, second = tile(q)[:H], tile(q)[H:]
            if lv:
                first, second = second, first
            if odd:
                first = swap(first)
            else:
                second = swap(second)
            ar_in[t] = jnp.where(left_h, first, second).astype(BF)

    for lv in (0, 1):
        pl.when(l == lv)(lambda lv=lv: pack(lv))

    for dc, dl in offs:
        t = lax.rem(c + dc, 4)
        o = 2 * dc + dl
        send(am_in.at[t], a4.at[x, rows(c, M1), main_lane(l)], S_AM + o, zdev(dc, dl))
        send(ar_in.at[t], arb.at[2 * c + l], S_AR + o, zdev(dc, dl))
    h0, h1 = pl.ds(0, H), pl.ds(H, H)

    def grow(block, half):
        return pl.ds(pl.multiple_of(block * M1 + half * H, 16), H)

    send(g_in.at[h0], gb.at[grow(c, 0)], S_G + 0, zdev(1, 0))
    send(g_in.at[h1], gb.at[grow(c, 1)], S_G + 1, zdev(3, 0))
    for i in (2, 1, 3):
        send(w_in, wb.at[rows(d, KB)], S_WY + i - 1, ydev(i))
    send(w_in, wb.at[rows(d, KB)], S_WC + 0, sib)
    send(g_in.at[h1], gb.at[grow(c, 1)], S_G + 2, zdev(1, 0))
    send(g_in.at[h0], gb.at[grow(c, 0)], S_G + 3, zdev(3, 0))

    own = [
        pltpu.make_async_copy(am_in.at[c], a4.at[x, rows(c, M1), main_lane(l)], ls.at[0]),
        pltpu.make_async_copy(ar_in.at[c], arb.at[2 * c + l], ls.at[1]),
        pltpu.make_async_copy(w_in, wb.at[rows(d, KB)], ls.at[2]),
        pltpu.make_async_copy(g_in, gb.at[rows(c, M1)], ls.at[3]),
    ]
    for cp in own:
        cp.start()
    own[0].wait()
    own[1].wait()

    for dc, dl in offs:
        cc, ll = lax.rem(c + 4 - dc, 4), lax.rem(l + dl, 2)
        o = 2 * dc + dl
        arrived(a4.at[x, rows(cc, M1), main_lane(ll)], S_AM + o, zdev(dc, dl))
        arrived(arb.at[2 * cc + ll], S_AR + o, zdev(dc, dl))
    for q in range(4):
        p0, p1 = arb[2 * q].astype(F32), arb[2 * q + 1].astype(F32)
        low = jnp.where(left_h, p0, p1)
        high = swap(jnp.where(left_h, p1, p0))
        a4[x, pl.ds(q * M1, H), pl.ds(128, 128)] = low.astype(BF)
        a4[x, pl.ds(q * M1 + H, H), pl.ds(128, 128)] = high.astype(BF)
    for i in (2, 1, 3):
        send(a4.at[x], a4.at[x], S_AX + i - 1, xdev(i))

    cl, cr, co = lax.rem(c + 3, 4), lax.rem(c + 1, 4), lax.rem(c + 2, 4)
    arrived(gb.at[grow(cl, 0)], S_G + 0, zdev(1, 0))
    send(gb.at[grow(cl, 0)], gb.at[grow(cl, 0)], S_G + 4, zdev(1, 0))
    arrived(gb.at[grow(cr, 1)], S_G + 1, zdev(3, 0))
    send(gb.at[grow(cr, 1)], gb.at[grow(cr, 1)], S_G + 5, zdev(3, 0))

    own[2].wait()
    own[3].wait()
    for i in (1, 3, 2):
        src = 2 * lax.rem(y + 4 - i, 4) + k
        arrived(wb.at[rows(src, KB)], S_WY + i - 1, ydev(i))
        send(wb.at[rows(src, KB)], wb.at[rows(src, KB)], S_WC + i, sib)

    for i in (1, 3, 2):
        src = lax.rem(x + 4 - i, 4)
        arrived(a4.at[src], S_AX + i - 1, xdev(i))
    for i in (0, 1, 3, 2):
        src = 2 * lax.rem(y + 4 - i, 4) + 1 - k
        arrived(wb.at[rows(src, KB)], S_WC + i, sib)

    def yrow(block, half):
        return pl.ds(pl.multiple_of(block * M1 + half * H, 16), H)

    for j in range(NJ):
        @pl.loop(0, NC // 256)
        def _(t):
            cols = pl.ds(pl.multiple_of(j * NC + t * 256, 256), 256)
            a = jnp.concatenate([a4[0], a4[1], a4[2], a4[3]], axis=1)
            yp[:, cols] = jnp.dot(a, wb[:, cols], preferred_element_type=F32)

        cols = pl.ds(j * NC, NC)
        for kind, block, half, dc in ((0, co, 0, 1), (1, co, 1, 3), (2, cr, 1, 1), (3, cl, 0, 3)):
            ysend[kind, j] = yp[yrow(block, half), cols].astype(BF)
            send(ysend.at[kind, j], yrecv.at[kind, j], S_Y + 3 * kind + j, zdev(dc, 0))

    for q in range(4):
        at4[q] = a4[q].T

    arrived(gb.at[grow(cl, 1)], S_G + 2, zdev(1, 0))
    arrived(gb.at[grow(cr, 0)], S_G + 3, zdev(3, 0))
    arrived(gb.at[grow(co, 0)], S_G + 4, zdev(1, 0))
    arrived(gb.at[grow(co, 1)], S_G + 5, zdev(3, 0))

    def nt_dot(a, b):
        return lax.dot_general(a, b, (((1,), (1,)), ((), ())), preferred_element_type=F32)

    for pair in ((2, 1), (3, 0)):
        xa, xb = lax.rem(x + pair[0], 4), lax.rem(x + pair[1], 4)
        wa = pl.multiple_of(xa * XB, 128)
        wc = pl.multiple_of(xb * XB, 128)
        g = gb[...]
        gs[pair[0], :, 0:256] = nt_dot(g, wb[pl.ds(wa, 256), :]).astype(BF)
        mid = jnp.concatenate([wb[pl.ds(wa + 256, 128), :], wb[pl.ds(wc, 128), :]], axis=0)
        mid = nt_dot(g, mid).astype(BF)
        gs[pair[0], :, 256:384] = mid[:, :128]
        gs[pair[1], :, 0:128] = mid[:, 128:]
        gs[pair[1], :, 128:384] = nt_dot(g, wb[pl.ds(wc + 128, 256), :]).astype(BF)
        for i in pair:
            if i:
                send(gs.at[i], grecv.at[i - 1], S_GX + i - 1, xdev(i))

    def relay(j):
        cols = pl.ds(j * NC, NC)
        arrived(yrecv.at[0, j], S_Y + j, zdev(1, 0))
        ysend[4, j] = (yp[yrow(cr, 0), cols] + yrecv[0, j].astype(F32)).astype(BF)
        send(ysend.at[4, j], yrecv.at[4, j], S_Y + 12 + j, zdev(1, 0))
        arrived(yrecv.at[1, j], S_Y + 3 + j, zdev(3, 0))
        ysend[5, j] = (yp[yrow(cl, 1), cols] + yrecv[1, j].astype(F32)).astype(BF)
        send(ysend.at[5, j], yrecv.at[5, j], S_Y + 15 + j, zdev(3, 0))

    for pair in ((2, 1), (3, 0)):
        ya, yb = lax.rem(y + pair[0], 4), lax.rem(y + pair[1], 4)

        @pl.loop(0, N // 256)
        def _(t):
            cols = pl.ds(pl.multiple_of(t * 256, 256), 256)
            at = jnp.concatenate([at4[ya], at4[yb]], axis=0)
            acc = jnp.dot(at, gb[:, cols], preferred_element_type=F32)
            for q in range(4):
                gw[2 * pair[q // 2] + q % 2, :, cols] = acc[q * KB : (q + 1) * KB]

        for i in pair:
            cs[i] = gw[2 * i + 1 - k].astype(BF)
            send(cs.at[i], crecv.at[i], S_CS + i, sib)

    def along_y(i):
        arrived(crecv.at[i], S_CS + i, sib)
        ws[i - 1] = (gw[2 * i + k] + crecv[i].astype(F32)).astype(BF)
        send(ws.at[i - 1], wrecv.at[i - 1], S_WS + i - 1, ydev(i))

    along_y(2)
    along_y(1)
    relay(0)
    along_y(3)
    relay(1)
    relay(2)
    arrived(crecv.at[0], S_CS + 0, sib)

    for i in (1, 3, 2):
        arrived(grecv.at[i - 1], S_GX + i - 1, xdev(i))
    total = gs[0].astype(F32) + grecv[0].astype(F32)
    total += grecv[1].astype(F32) + grecv[2].astype(F32)
    sx[...] = total.astype(BF)
    for q in range(4):
        t0 = sx[pl.ds(q * M1, H), pl.ds(128, 128)].astype(F32)
        t1 = swap(sx[pl.ds(q * M1 + H, H), pl.ds(128, 128)].astype(F32))
        srem[2 * q] = jnp.where(left_h, t0, t1).astype(BF)
        srem[2 * q + 1] = jnp.where(left_h, t1, t0).astype(BF)
    for dc, dl in offs:
        cc, ll = lax.rem(c + dc, 4), lax.rem(l + dl, 2)
        o = 2 * dc + dl
        send(sx.at[rows(cc, M1), main_lane(ll)], fm.at[2 * c + l], S_GM + o, zdev(dc, dl))
        send(srem.at[2 * cc + ll], fr.at[2 * c + l], S_GR + o, zdev(dc, dl))
    fm[2 * c + l] = sx[rows(c, M1), main_lane(l)]
    fr[2 * c + l] = srem[2 * c + l]

    for j in range(NJ):
        cols = pl.ds(j * NC, NC)
        for kind, dc in ((2, 1), (3, 3), (4, 1), (5, 3)):
            arrived(yrecv.at[kind, j], S_Y + 3 * kind + j, zdev(dc, 0))
        y_out[h0, cols] = (
            yp[yrow(c, 0), cols] + yrecv[4, j].astype(F32) + yrecv[3, j].astype(F32)
        ).astype(BF)
        y_out[h1, cols] = (
            yp[yrow(c, 1), cols] + yrecv[5, j].astype(F32) + yrecv[2, j].astype(F32)
        ).astype(BF)

    for i in (1, 3, 2):
        arrived(wrecv.at[i - 1], S_WS + i - 1, ydev(i))
    w_out[...] = (
        gw[k] + crecv[0].astype(F32)
        + wrecv[0].astype(F32) + wrecv[1].astype(F32) + wrecv[2].astype(F32)
    ).astype(BF)

    for dc, dl in offs:
        cc, ll = lax.rem(c + 4 - dc, 4), lax.rem(l + dl, 2)
        o = 2 * dc + dl
        arrived(fm.at[2 * cc + ll], S_GM + o, zdev(dc, dl))
        arrived(fr.at[2 * cc + ll], S_GR + o, zdev(dc, dl))

    def unpack(lv):
        units = []
        for t in range(4):
            m = fm[2 * t].astype(F32) + fm[2 * t + 1].astype(F32)
            p = fr[2 * t].astype(F32) + fr[2 * t + 1].astype(F32)
            halves = [swap(p), p] if lv else [p, swap(p)]
            rem = (jnp.concatenate(halves, axis=0), jnp.concatenate(halves[::-1], axis=0))
            main = [(m, swap(m)), (swap(m), m)]
            units += [rem] + main if lv else main + [rem]
        for q in range(6):
            ga_out[:, 128 * q : 128 * q + 128] = jnp.where(
                left, units[2 * q][0], units[2 * q + 1][1]
            ).astype(BF)

    for lv in (0, 1):
        pl.when(l == lv)(lambda lv=lv: unpack(lv))

    for cp in pending:
        cp.wait_send()


def per_device(acts, w_out, grad_out):
    def vm(shape, dtype=BF):
        return pltpu.VMEM(shape, dtype)

    return pl.pallas_call(
        kernel,
        out_shape=[vm((M1, N)), vm((M1, 4 * KB)), vm((KB, N))],
        in_specs=[
            pl.BlockSpec(memory_space=pltpu.VMEM),
            pl.BlockSpec(memory_space=pltpu.HBM),
            pl.BlockSpec(memory_space=pltpu.HBM),
        ],
        out_specs=[pl.BlockSpec(memory_space=pltpu.VMEM)] * 3,
        scratch_shapes=[
            vm((4, M1, 128)),
            vm((4, H, 128)),
            vm((4, MG, XB)),
            vm((8, H, 128)),
            vm((N, N)),
            vm((MG, N)),
            vm((4, XB, MG)),
            vm((MG, N), F32),
            vm((6, NJ, H, NC)),
            vm((6, NJ, H, NC)),
            vm((4, MG, XB)),
            vm((3, MG, XB)),
            vm((MG, XB)),
            vm((8, H, 128)),
            vm((8, M1, 128)),
            vm((8, H, 128)),
            vm((8, KB, N), F32),
            vm((4, KB, N)),
            vm((4, KB, N)),
            vm((3, KB, N)),
            vm((3, KB, N)),
            pltpu.SemaphoreType.DMA((N_SEM,)),
            pltpu.SemaphoreType.DMA((N_SEM,)),
            pltpu.SemaphoreType.DMA((4,)),
        ],
        compiler_params=pltpu.CompilerParams(
            collective_id=0, has_side_effects=True, vmem_limit_bytes=50 * 2**20
        ),
        cost_estimate=pl.CostEstimate(
            flops=6 * MG * N * N, bytes_accessed=3 * 2**20, transcendentals=0
        ),
    )(acts, w_out, grad_out)


def solution(mesh):
    spec = P(("depth", "col"), "row")
    return jax.shard_map(
        per_device, mesh=mesh, in_specs=(spec,) * 3, out_specs=(spec,) * 3, check_vma=False
    )
```

```python
import jax
import jax.numpy as jnp
from jax import lax
from jax.experimental import pallas as pl
from jax.experimental.pallas import tpu as pltpu
from jax.sharding import PartitionSpec as P

MESH = pl.DeviceIdType.MESH
BF = jnp.bfloat16
F32 = jnp.float32

M1 = 160
MG = 640
KB = 192
XB = 384
N = 1536
H = 80
NC = 512
NJ = N // NC

S_AM, S_AR, S_AX, S_WY, S_WC, S_G, S_Y, S_GX, S_GM, S_GR, S_CS, S_WS = (
    0, 8, 16, 28, 34, 41, 47, 65, 68, 76, 84, 88,
)
N_SEM = 91


def kernel(
    acts_in, w_in, g_in,
    y_out, ga_out, w_out,
    acts, am_in, a4, arm, wb, gb, at4, yp, ysend, yrecv, gs, grecv, sz, fz,
    gw, cs, crecv, ws, wrecv, ss, rs, ls,
):
    d, r, c = lax.axis_index("depth"), lax.axis_index("row"), lax.axis_index("col")
    y, k = d // 2, lax.rem(d, 2)
    x, l = r // 2, lax.rem(r, 2)

    def xdev(i):
        return (d, 2 * lax.rem(x + i, 4) + l, c)

    def ydev(i):
        return (2 * lax.rem(y + i, 4) + k, r, c)

    def zdev(dc, dl):
        return (d, 2 * x + lax.rem(l + dl, 2), lax.rem(c + dc, 4))

    sib = (2 * y + 1 - k, r, c)
    offs = [(dc, dl) for dc in (2, 1, 3, 0) for dl in (0, 1) if (dc, dl) != (0, 0)]

    load = pltpu.make_async_copy(acts_in, acts, ls.at[3])
    load.start()
    bar = pltpu.get_barrier_semaphore()
    peers = [zdev(*o) for o in offs] + [xdev(i) for i in (1, 2, 3)]
    peers += [ydev(i) for i in (1, 2, 3)] + [sib]
    for p in peers:
        pl.semaphore_signal(bar, inc=1, device_id=p, device_id_type=MESH)

    pending = []

    def copy(src, dst, sem, dev):
        return pltpu.make_async_remote_copy(
            src, dst, ss.at[sem], rs.at[sem], device_id=dev, device_id_type=MESH
        )

    def send(src, dst, sem, dev):
        cp = copy(src, dst, sem, dev)
        cp.start()
        pending.append(cp)

    def arrived(dst, sem, dev):
        copy(dst, dst, sem, dev).wait_recv()

    def rows(i, size):
        return pl.ds(pl.multiple_of(i * size, 16), size)

    lane = lax.broadcasted_iota(jnp.int32, (M1, 128), 1)
    left = lane < 64
    left_h = left[:H]

    def swap(v):
        return pltpu.roll(v, 64, 1)

    def pack(lv):
        def tile(q):
            return acts[:, 128 * q : 128 * q + 128].astype(F32)

        for t in range(4):
            q, odd = divmod(KB * t + 64 * lv, 128)
            if odd:
                am_in[t, :M1] = swap(jnp.where(left, tile(q + 1), tile(q))).astype(BF)
            else:
                am_in[t, :M1] = acts[:, 128 * q : 128 * q + 128]
            q, odd = divmod(KB * t + 128 * (1 - lv), 128)
            first, second = tile(q)[:H], tile(q)[H:]
            if lv:
                first, second = second, first
            if odd:
                first = swap(first)
            else:
                second = swap(second)
            am_in[t, M1:] = jnp.where(left_h, first, second).astype(BF)

    load.wait()
    for lv in (0, 1):
        pl.when(l == lv)(lambda lv=lv: pack(lv))
    pl.semaphore_wait(bar, len(peers))

    for dc, dl in offs:
        t = lax.rem(c + dc, 4)
        o = 2 * dc + dl
        send(am_in.at[t], arm.at[2 * c + l], S_AM + o, zdev(dc, dl))
    h0, h1 = pl.ds(0, H), pl.ds(H, H)

    def grow(block, half):
        return pl.ds(pl.multiple_of(block * M1 + half * H, 16), H)

    send(g_in.at[h0], gb.at[grow(c, 0)], S_G + 0, zdev(1, 0))
    send(g_in.at[h1], gb.at[grow(c, 1)], S_G + 1, zdev(3, 0))
    def wrow(block, half):
        return pl.ds(pl.multiple_of(block * KB + half * (KB // 2), 16), KB // 2)

    w0, w1 = pl.ds(0, KB // 2), pl.ds(KB // 2, KB // 2)
    send(w_in.at[w0], wb.at[wrow(d, 0)], S_WY + 0, ydev(1))
    send(w_in.at[w1], wb.at[wrow(d, 1)], S_WY + 1, ydev(3))
    send(w_in.at[w1], wb.at[wrow(d, 1)], S_WY + 2, ydev(1))
    send(w_in.at[w0], wb.at[wrow(d, 0)], S_WY + 3, ydev(3))
    send(w_in, wb.at[rows(d, KB)], S_WC + 6, sib)
    send(g_in.at[h1], gb.at[grow(c, 1)], S_G + 2, zdev(1, 0))
    send(g_in.at[h0], gb.at[grow(c, 0)], S_G + 3, zdev(3, 0))

    own = [
        pltpu.make_async_copy(am_in.at[c], arm.at[2 * c + l], ls.at[0]),
        pltpu.make_async_copy(w_in, wb.at[rows(d, KB)], ls.at[1]),
        pltpu.make_async_copy(g_in, gb.at[rows(c, M1)], ls.at[2]),
    ]
    for cp in own:
        cp.start()
    own[0].wait()

    y_l, y_r, y_o = (2 * lax.rem(y + i, 4) + k for i in (3, 1, 2))

    def pass_w(block, half, sem):
        place = wb.at[wrow(block, half)]
        arrived(place, S_WY + sem, sib)
        if sem < 2:
            send(place, place, S_WY + 4 + sem, ydev(1 + 2 * sem))
        send(place, place, S_WC + sem, sib)

    pass_w(y_l, 0, 0)
    pass_w(y_r, 1, 1)

    x_l, x_r, x_o = (lax.rem(x + i, 4) for i in (3, 1, 2))
    order = (0, 1, 3, 2)
    for n, step in enumerate(order):
        q = lax.rem(c + step, 4)
        dc = (4 - step) % 4
        for dl in (0, 1):
            if (dc, dl) != (0, 0):
                ll = lax.rem(l + dl, 2)
                o = 2 * dc + dl
                arrived(arm.at[2 * q + ll], S_AM + o, sib)
        a4[x, rows(q, M1), 0:128] = arm[2 * q, :M1]
        a4[x, rows(q, M1), 256:384] = arm[2 * q + 1, :M1]
        p0, p1 = arm[2 * q, M1:].astype(F32), arm[2 * q + 1, M1:].astype(F32)
        low = jnp.where(left_h, p0, p1)
        high = swap(jnp.where(left_h, p1, p0))
        a4[x, grow(q, 0), pl.ds(128, 128)] = low.astype(BF)
        a4[x, grow(q, 1), pl.ds(128, 128)] = high.astype(BF)
        place = a4.at[x, rows(q, M1)]
        send(place, place, S_AX + n, xdev(1))
        send(place, place, S_AX + 4 + n, xdev(3))

    cl, cr, co = lax.rem(c + 3, 4), lax.rem(c + 1, 4), lax.rem(c + 2, 4)
    arrived(gb.at[grow(cl, 0)], S_G + 0, zdev(1, 0))
    send(gb.at[grow(cl, 0)], gb.at[grow(cl, 0)], S_G + 4, zdev(1, 0))
    arrived(gb.at[grow(cr, 1)], S_G + 1, zdev(3, 0))
    send(gb.at[grow(cr, 1)], gb.at[grow(cr, 1)], S_G + 5, zdev(3, 0))

    pass_w(y_l, 1, 2)
    pass_w(y_r, 0, 3)

    own[1].wait()
    own[2].wait()

    def a_rows(xs, n):
        return a4.at[xs, rows(lax.rem(c + order[n], 4), M1)]

    for n in (0, 2, 1, 3):
        xs, sem, to = (x_l, n, 1) if n < 2 else (x_r, 4 + n, 3)
        place = a_rows(xs, n)
        arrived(place, S_AX + sem, sib)
        send(place, place, S_AX + 8 + n, xdev(to))

    pass_w(y_o, 0, 4)
    pass_w(y_o, 1, 5)

    for n in range(4):
        xs, sem = (x_r, 4 + n) if n < 2 else (x_l, n)
        arrived(a_rows(xs, n), S_AX + sem, sib)
    for n in range(4):
        arrived(a_rows(x_o, n), S_AX + 8 + n, sib)
    arrived(wb.at[rows(2 * y + 1 - k, KB)], S_WC + 6, sib)
    flip = 1 - 2 * k
    for sem, (block, half) in enumerate(
        ((y_l, 0), (y_r, 1), (y_l, 1), (y_r, 0), (y_o, 0), (y_o, 1))
    ):
        arrived(wb.at[wrow(block + flip, half)], S_WC + sem, sib)

    def yrow(block, half):
        return pl.ds(pl.multiple_of(block * M1 + half * H, 16), H)

    for j in range(NJ):
        @pl.loop(0, NC // 256)
        def _(t):
            cols = pl.ds(pl.multiple_of(j * NC + t * 256, 256), 256)
            a = jnp.concatenate([a4[0], a4[1], a4[2], a4[3]], axis=1)
            yp[:, cols] = jnp.dot(a, wb[:, cols], preferred_element_type=F32)

        cols = pl.ds(j * NC, NC)
        for kind, block, half in ((0, co, 0), (1, co, 1), (2, cr, 1), (3, cl, 0)):
            ysend[kind, j] = yp[yrow(block, half), cols].astype(BF)

    for q in range(4):
        at4[q] = a4[q].T

    arrived(gb.at[grow(cl, 1)], S_G + 2, zdev(1, 0))
    arrived(gb.at[grow(cr, 0)], S_G + 3, zdev(3, 0))
    arrived(gb.at[grow(co, 0)], S_G + 4, zdev(1, 0))
    arrived(gb.at[grow(co, 1)], S_G + 5, zdev(3, 0))

    def send_y(first):
        for j in range(NJ):
            for kind, dc in ((first, 1), (first + 1, 3)):
                send(ysend.at[kind, j], yrecv.at[kind, j], S_Y + 3 * kind + j, zdev(dc, 0))

    send_y(0)
    send_y(2)

    def nt_dot(a, b):
        return lax.dot_general(a, b, (((1,), (1,)), ((), ())), preferred_element_type=F32)

    for pair in ((2, 1), (3, 0)):
        xa, xb = lax.rem(x + pair[0], 4), lax.rem(x + pair[1], 4)
        wa = pl.multiple_of(xa * XB, 128)
        wc = pl.multiple_of(xb * XB, 128)
        g = gb[...]
        gs[pair[0], :, 0:256] = nt_dot(g, wb[pl.ds(wa, 256), :]).astype(BF)
        mid = jnp.concatenate([wb[pl.ds(wa + 256, 128), :], wb[pl.ds(wc, 128), :]], axis=0)
        mid = nt_dot(g, mid).astype(BF)
        gs[pair[0], :, 256:384] = mid[:, :128]
        gs[pair[1], :, 0:128] = mid[:, 128:]
        gs[pair[1], :, 128:384] = nt_dot(g, wb[pl.ds(wc + 128, 256), :]).astype(BF)
        for i in pair:
            if i:
                send(gs.at[i], grecv.at[i - 1], S_GX + i - 1, xdev(i))

    def relay(j):
        cols = pl.ds(j * NC, NC)
        arrived(yrecv.at[0, j], S_Y + j, zdev(1, 0))
        ysend[4, j] = (yp[yrow(cr, 0), cols] + yrecv[0, j].astype(F32)).astype(BF)
        send(ysend.at[4, j], yrecv.at[4, j], S_Y + 12 + j, zdev(1, 0))
        arrived(yrecv.at[1, j], S_Y + 3 + j, zdev(3, 0))
        ysend[5, j] = (yp[yrow(cl, 1), cols] + yrecv[1, j].astype(F32)).astype(BF)
        send(ysend.at[5, j], yrecv.at[5, j], S_Y + 15 + j, zdev(3, 0))

    for pair in ((2, 1), (3, 0)):
        ya, yb = lax.rem(y + pair[0], 4), lax.rem(y + pair[1], 4)

        @pl.loop(0, N // 256)
        def _(t):
            cols = pl.ds(pl.multiple_of(t * 256, 256), 256)
            at = jnp.concatenate([at4[ya], at4[yb]], axis=0)
            acc = jnp.dot(at, gb[:, cols], preferred_element_type=F32)
            for q in range(4):
                gw[2 * pair[q // 2] + q % 2, :, cols] = acc[q * KB : (q + 1) * KB]

        for i in pair:
            cs[i] = gw[2 * i + 1 - k].astype(BF)
            send(cs.at[i], crecv.at[i], S_CS + i, sib)

    def along_y(i):
        arrived(crecv.at[i], S_CS + i, sib)
        ws[i - 1] = (gw[2 * i + k] + crecv[i].astype(F32)).astype(BF)
        send(ws.at[i - 1], wrecv.at[i - 1], S_WS + i - 1, ydev(i))

    along_y(2)
    along_y(1)
    relay(0)
    along_y(3)
    relay(1)
    relay(2)
    arrived(crecv.at[0], S_CS + 0, sib)

    for i in (1, 3, 2):
        arrived(grecv.at[i - 1], S_GX + i - 1, xdev(i))
    total = gs[0].astype(F32) + grecv[0].astype(F32)
    total += grecv[1].astype(F32) + grecv[2].astype(F32)
    for q in range(4):
        for ll in (0, 1):
            sz[2 * q + ll, :M1] = total[q * M1 : (q + 1) * M1, 256 * ll : 256 * ll + 128].astype(BF)
        t0 = total[q * M1 : q * M1 + H, 128:256]
        t1 = swap(total[q * M1 + H : (q + 1) * M1, 128:256])
        sz[2 * q, M1:] = jnp.where(left_h, t0, t1).astype(BF)
        sz[2 * q + 1, M1:] = jnp.where(left_h, t1, t0).astype(BF)
    for dc, dl in offs:
        cc, ll = lax.rem(c + dc, 4), lax.rem(l + dl, 2)
        send(sz.at[2 * cc + ll], fz.at[2 * c + l], S_GM + 2 * dc + dl, zdev(dc, dl))
    fz[2 * c + l] = sz[2 * c + l]

    for j in range(NJ):
        cols = pl.ds(j * NC, NC)
        for kind, dc in ((2, 1), (3, 3), (4, 1), (5, 3)):
            arrived(yrecv.at[kind, j], S_Y + 3 * kind + j, zdev(dc, 0))
        y_out[h0, cols] = (
            yp[yrow(c, 0), cols] + yrecv[4, j].astype(F32) + yrecv[3, j].astype(F32)
        ).astype(BF)
        y_out[h1, cols] = (
            yp[yrow(c, 1), cols] + yrecv[5, j].astype(F32) + yrecv[2, j].astype(F32)
        ).astype(BF)

    for i in (1, 3, 2):
        arrived(wrecv.at[i - 1], S_WS + i - 1, ydev(i))
    w_out[...] = (
        gw[k] + crecv[0].astype(F32)
        + wrecv[0].astype(F32) + wrecv[1].astype(F32) + wrecv[2].astype(F32)
    ).astype(BF)

    for dc, dl in offs:
        cc, ll = lax.rem(c + 4 - dc, 4), lax.rem(l + dl, 2)
        o = 2 * dc + dl
        arrived(fz.at[2 * cc + ll], S_GM + o, zdev(dc, dl))

    def unpack(lv):
        units = []
        for t in range(4):
            f = fz[2 * t].astype(F32) + fz[2 * t + 1].astype(F32)
            m, p = f[:M1], f[M1:]
            halves = [swap(p), p] if lv else [p, swap(p)]
            rem = (jnp.concatenate(halves, axis=0), jnp.concatenate(halves[::-1], axis=0))
            main = [(m, swap(m)), (swap(m), m)]
            units += [rem] + main if lv else main + [rem]
        for q in range(6):
            ga_out[:, 128 * q : 128 * q + 128] = jnp.where(
                left, units[2 * q][0], units[2 * q + 1][1]
            ).astype(BF)

    for lv in (0, 1):
        pl.when(l == lv)(lambda lv=lv: unpack(lv))

    for cp in pending:
        cp.wait_send()


def per_device(acts, w_out, grad_out):
    def vm(shape, dtype=BF):
        return pltpu.VMEM(shape, dtype)

    return pl.pallas_call(
        kernel,
        out_shape=[vm((M1, N)), vm((M1, 4 * KB)), vm((KB, N))],
        in_specs=[
            pl.BlockSpec(memory_space=pltpu.HBM),
            pl.BlockSpec(memory_space=pltpu.HBM),
            pl.BlockSpec(memory_space=pltpu.HBM),
        ],
        out_specs=[pl.BlockSpec(memory_space=pltpu.VMEM)] * 3,
        scratch_shapes=[
            vm((M1, 4 * KB)),
            vm((4, M1 + H, 128)),
            vm((4, MG, XB)),
            vm((8, M1 + H, 128)),
            vm((N, N)),
            vm((MG, N)),
            vm((4, XB, MG)),
            vm((MG, N), F32),
            vm((6, NJ, H, NC)),
            vm((6, NJ, H, NC)),
            vm((4, MG, XB)),
            vm((3, MG, XB)),
            vm((8, M1 + H, 128)),
            vm((8, M1 + H, 128)),
            vm((8, KB, N), F32),
            vm((4, KB, N)),
            vm((4, KB, N)),
            vm((3, KB, N)),
            vm((3, KB, N)),
            pltpu.SemaphoreType.DMA((N_SEM,)),
            pltpu.SemaphoreType.DMA((N_SEM,)),
            pltpu.SemaphoreType.DMA((4,)),
        ],
        compiler_params=pltpu.CompilerParams(
            collective_id=0, has_side_effects=True, vmem_limit_bytes=62 * 2**20
        ),
        cost_estimate=pl.CostEstimate(
            flops=6 * MG * N * N, bytes_accessed=3 * 2**20, transcendentals=0
        ),
    )(acts, w_out, grad_out)


def solution(mesh):
    spec = P(("depth", "col"), "row")
    return jax.shard_map(
        per_device, mesh=mesh, in_specs=(spec,) * 3, out_specs=(spec,) * 3, check_vma=False
    )
```

```python
import jax
import jax.numpy as jnp
from jax import lax
from jax.experimental import pallas as pl
from jax.experimental.pallas import tpu as pltpu
from jax.sharding import PartitionSpec as P

MESH = pl.DeviceIdType.MESH
BF = jnp.bfloat16
F32 = jnp.float32

M1 = 160
MG = 640
KB = 192
XB = 384
N = 1536
H = 80
NC = 512
NJ = N // NC

S_AM, S_AR, S_AX, S_WY, S_WC, S_G, S_Y, S_GX, S_GM, S_GR, S_CS, S_WS = (
    0, 8, 16, 28, 34, 41, 47, 65, 68, 76, 84, 88,
)
N_SEM = 91


def kernel(
    acts_in, w_in, g_in,
    y_out, ga_out, w_out,
    acts, am_in, a4, arm, wb, gb, at4, yp, ysend, yrecv, gs, grecv, sz, fz,
    gw, cs, crecv, ws, wrecv, ss, rs, ls,
):
    d, r, c = lax.axis_index("depth"), lax.axis_index("row"), lax.axis_index("col")
    y, k = d // 2, lax.rem(d, 2)
    x, l = r // 2, lax.rem(r, 2)

    def xdev(i):
        return (d, 2 * lax.rem(x + i, 4) + l, c)

    def ydev(i):
        return (2 * lax.rem(y + i, 4) + k, r, c)

    def zdev(dc, dl):
        return (d, 2 * x + lax.rem(l + dl, 2), lax.rem(c + dc, 4))

    sib = (2 * y + 1 - k, r, c)
    offs = [(dc, dl) for dc in (2, 1, 3, 0) for dl in (0, 1) if (dc, dl) != (0, 0)]

    load = pltpu.make_async_copy(acts_in, acts, ls.at[3])
    load.start()
    bar = pltpu.get_barrier_semaphore()
    peers = [zdev(*o) for o in offs] + [xdev(i) for i in (1, 2, 3)]
    peers += [ydev(i) for i in (1, 2, 3)] + [sib]
    for p in peers:
        pl.semaphore_signal(bar, inc=1, device_id=p, device_id_type=MESH)

    pending = []

    def copy(src, dst, sem, dev):
        return pltpu.make_async_remote_copy(
            src, dst, ss.at[sem], rs.at[sem], device_id=dev, device_id_type=MESH
        )

    def send(src, dst, sem, dev):
        cp = copy(src, dst, sem, dev)
        cp.start()
        pending.append(cp)

    def arrived(dst, sem, dev):
        copy(dst, dst, sem, dev).wait_recv()

    def rows(i, size):
        return pl.ds(pl.multiple_of(i * size, 16), size)

    lane = lax.broadcasted_iota(jnp.int32, (M1, 128), 1)
    left = lane < 64
    left_h = left[:H]

    def swap(v):
        return pltpu.roll(v, 64, 1)

    def pack(lv):
        def tile(q):
            return acts[:, 128 * q : 128 * q + 128].astype(F32)

        for t in range(4):
            q, odd = divmod(KB * t + 64 * lv, 128)
            if odd:
                am_in[t, :M1] = swap(jnp.where(left, tile(q + 1), tile(q))).astype(BF)
            else:
                am_in[t, :M1] = acts[:, 128 * q : 128 * q + 128]
            q, odd = divmod(KB * t + 128 * (1 - lv), 128)
            first, second = tile(q)[:H], tile(q)[H:]
            if lv:
                first, second = second, first
            if odd:
                first = swap(first)
            else:
                second = swap(second)
            am_in[t, M1:] = jnp.where(left_h, first, second).astype(BF)

    load.wait()
    for lv in (0, 1):
        pl.when(l == lv)(lambda lv=lv: pack(lv))
    pl.semaphore_wait(bar, len(peers))

    for dc, dl in offs:
        t = lax.rem(c + dc, 4)
        o = 2 * dc + dl
        send(am_in.at[t], arm.at[2 * c + l], S_AM + o, zdev(dc, dl))
    h0, h1 = pl.ds(0, H), pl.ds(H, H)

    def grow(block, half):
        return pl.ds(pl.multiple_of(block * M1 + half * H, 16), H)

    send(g_in.at[h0], gb.at[grow(c, 0)], S_G + 0, zdev(1, 0))
    send(g_in.at[h1], gb.at[grow(c, 1)], S_G + 1, zdev(3, 0))
    def wrow(block, half):
        return pl.ds(pl.multiple_of(block * KB + half * (KB // 2), 16), KB // 2)

    w0, w1 = pl.ds(0, KB // 2), pl.ds(KB // 2, KB // 2)
    send(w_in.at[w0], wb.at[wrow(d, 0)], S_WY + 0, ydev(1))
    send(w_in.at[w1], wb.at[wrow(d, 1)], S_WY + 1, ydev(3))
    send(w_in.at[w1], wb.at[wrow(d, 1)], S_WY + 2, ydev(1))
    send(w_in.at[w0], wb.at[wrow(d, 0)], S_WY + 3, ydev(3))
    send(w_in, wb.at[rows(d, KB)], S_WC + 6, sib)
    send(g_in.at[h1], gb.at[grow(c, 1)], S_G + 2, zdev(1, 0))
    send(g_in.at[h0], gb.at[grow(c, 0)], S_G + 3, zdev(3, 0))

    own = [
        pltpu.make_async_copy(am_in.at[c], arm.at[2 * c + l], ls.at[0]),
        pltpu.make_async_copy(w_in, wb.at[rows(d, KB)], ls.at[1]),
        pltpu.make_async_copy(g_in, gb.at[rows(c, M1)], ls.at[2]),
    ]
    for cp in own:
        cp.start()
    own[0].wait()

    y_l, y_r, y_o = (2 * lax.rem(y + i, 4) + k for i in (3, 1, 2))

    def pass_w(block, half, sem):
        place = wb.at[wrow(block, half)]
        arrived(place, S_WY + sem, sib)
        if sem < 2:
            send(place, place, S_WY + 4 + sem, ydev(1 + 2 * sem))
        send(place, place, S_WC + sem, sib)

    pass_w(y_l, 0, 0)
    pass_w(y_r, 1, 1)

    x_l, x_r, x_o = (lax.rem(x + i, 4) for i in (3, 1, 2))
    order = (0, 1, 3, 2)
    for n, step in enumerate(order):
        q = lax.rem(c + step, 4)
        dc = (4 - step) % 4
        for dl in (0, 1):
            if (dc, dl) != (0, 0):
                ll = lax.rem(l + dl, 2)
                o = 2 * dc + dl
                arrived(arm.at[2 * q + ll], S_AM + o, sib)
        a4[x, rows(q, M1), 0:128] = arm[2 * q, :M1]
        a4[x, rows(q, M1), 256:384] = arm[2 * q + 1, :M1]
        p0, p1 = arm[2 * q, M1:].astype(F32), arm[2 * q + 1, M1:].astype(F32)
        low = jnp.where(left_h, p0, p1)
        high = swap(jnp.where(left_h, p1, p0))
        a4[x, grow(q, 0), pl.ds(128, 128)] = low.astype(BF)
        a4[x, grow(q, 1), pl.ds(128, 128)] = high.astype(BF)
        place = a4.at[x, rows(q, M1)]
        send(place, place, S_AX + n, xdev(1))
        send(place, place, S_AX + 4 + n, xdev(3))

    cl, cr, co = lax.rem(c + 3, 4), lax.rem(c + 1, 4), lax.rem(c + 2, 4)
    arrived(gb.at[grow(cl, 0)], S_G + 0, zdev(1, 0))
    send(gb.at[grow(cl, 0)], gb.at[grow(cl, 0)], S_G + 4, zdev(1, 0))
    arrived(gb.at[grow(cr, 1)], S_G + 1, zdev(3, 0))
    send(gb.at[grow(cr, 1)], gb.at[grow(cr, 1)], S_G + 5, zdev(3, 0))

    pass_w(y_l, 1, 2)
    pass_w(y_r, 0, 3)

    own[1].wait()
    own[2].wait()

    def a_rows(xs, n):
        return a4.at[xs, rows(lax.rem(c + order[n], 4), M1)]

    for n in (0, 2, 1, 3):
        xs, sem, to = (x_l, n, 1) if n < 2 else (x_r, 4 + n, 3)
        place = a_rows(xs, n)
        arrived(place, S_AX + sem, sib)
        send(place, place, S_AX + 8 + n, xdev(to))

    pass_w(y_o, 0, 4)
    pass_w(y_o, 1, 5)

    for n in range(4):
        xs, sem = (x_r, 4 + n) if n < 2 else (x_l, n)
        arrived(a_rows(xs, n), S_AX + sem, sib)
    for n in range(4):
        arrived(a_rows(x_o, n), S_AX + 8 + n, sib)
    arrived(wb.at[rows(2 * y + 1 - k, KB)], S_WC + 6, sib)
    flip = 1 - 2 * k
    for sem, (block, half) in enumerate(
        ((y_l, 0), (y_r, 1), (y_l, 1), (y_r, 0), (y_o, 0), (y_o, 1))
    ):
        arrived(wb.at[wrow(block + flip, half)], S_WC + sem, sib)

    def yrow(block, half):
        return pl.ds(pl.multiple_of(block * M1 + half * H, 16), H)

    for j in range(NJ):
        @pl.loop(0, NC // 256)
        def _(t):
            cols = pl.ds(pl.multiple_of(j * NC + t * 256, 256), 256)
            a = jnp.concatenate([a4[0], a4[1], a4[2], a4[3]], axis=1)
            yp[:, cols] = jnp.dot(a, wb[:, cols], preferred_element_type=F32)

        cols = pl.ds(j * NC, NC)
        for kind, block, half in ((0, co, 0), (1, co, 1), (2, cr, 1), (3, cl, 0)):
            ysend[kind, j] = yp[yrow(block, half), cols].astype(BF)

    for q in range(4):
        at4[q] = a4[q].T

    arrived(gb.at[grow(cl, 1)], S_G + 2, zdev(1, 0))
    arrived(gb.at[grow(cr, 0)], S_G + 3, zdev(3, 0))
    arrived(gb.at[grow(co, 0)], S_G + 4, zdev(1, 0))
    arrived(gb.at[grow(co, 1)], S_G + 5, zdev(3, 0))

    def send_y(first):
        for j in range(NJ):
            for kind, dc in ((first, 1), (first + 1, 3)):
                send(ysend.at[kind, j], yrecv.at[kind, j], S_Y + 3 * kind + j, zdev(dc, 0))

    send_y(0)

    def nt_dot(a, b):
        return lax.dot_general(a, b, (((1,), (1,)), ((), ())), preferred_element_type=F32)

    for pair in ((2, 1), (3, 0)):
        xa, xb = lax.rem(x + pair[0], 4), lax.rem(x + pair[1], 4)
        wa = pl.multiple_of(xa * XB, 128)
        wc = pl.multiple_of(xb * XB, 128)
        g = gb[...]
        gs[pair[0], :, 0:256] = nt_dot(g, wb[pl.ds(wa, 256), :]).astype(BF)
        mid = jnp.concatenate([wb[pl.ds(wa + 256, 128), :], wb[pl.ds(wc, 128), :]], axis=0)
        mid = nt_dot(g, mid).astype(BF)
        gs[pair[0], :, 256:384] = mid[:, :128]
        gs[pair[1], :, 0:128] = mid[:, 128:]
        gs[pair[1], :, 128:384] = nt_dot(g, wb[pl.ds(wc + 128, 256), :]).astype(BF)
        for i in pair:
            if i:
                send(gs.at[i], grecv.at[i - 1], S_GX + i - 1, xdev(i))

    send_y(2)

    def relay(j):
        cols = pl.ds(j * NC, NC)
        arrived(yrecv.at[0, j], S_Y + j, zdev(1, 0))
        ysend[4, j] = (yp[yrow(cr, 0), cols] + yrecv[0, j].astype(F32)).astype(BF)
        send(ysend.at[4, j], yrecv.at[4, j], S_Y + 12 + j, zdev(1, 0))
        arrived(yrecv.at[1, j], S_Y + 3 + j, zdev(3, 0))
        ysend[5, j] = (yp[yrow(cl, 1), cols] + yrecv[1, j].astype(F32)).astype(BF)
        send(ysend.at[5, j], yrecv.at[5, j], S_Y + 15 + j, zdev(3, 0))

    for pair in ((2, 1), (3, 0)):
        ya, yb = lax.rem(y + pair[0], 4), lax.rem(y + pair[1], 4)

        @pl.loop(0, N // 256)
        def _(t):
            cols = pl.ds(pl.multiple_of(t * 256, 256), 256)
            at = jnp.concatenate([at4[ya], at4[yb]], axis=0)
            acc = jnp.dot(at, gb[:, cols], preferred_element_type=F32)
            for q in range(4):
                gw[2 * pair[q // 2] + q % 2, :, cols] = acc[q * KB : (q + 1) * KB]

        for i in pair:
            cs[i] = gw[2 * i + 1 - k].astype(BF)
            send(cs.at[i], crecv.at[i], S_CS + i, sib)

    def along_y(i):
        arrived(crecv.at[i], S_CS + i, sib)
        ws[i - 1] = (gw[2 * i + k] + crecv[i].astype(F32)).astype(BF)
        send(ws.at[i - 1], wrecv.at[i - 1], S_WS + i - 1, ydev(i))

    along_y(2)
    relay(0)
    relay(1)
    relay(2)
    along_y(1)
    along_y(3)
    arrived(crecv.at[0], S_CS + 0, sib)

    for i in (1, 3, 2):
        arrived(grecv.at[i - 1], S_GX + i - 1, xdev(i))
    total = gs[0].astype(F32) + grecv[0].astype(F32)
    total += grecv[1].astype(F32) + grecv[2].astype(F32)
    for q in range(4):
        for ll in (0, 1):
            sz[2 * q + ll, :M1] = total[q * M1 : (q + 1) * M1, 256 * ll : 256 * ll + 128].astype(BF)
        t0 = total[q * M1 : q * M1 + H, 128:256]
        t1 = swap(total[q * M1 + H : (q + 1) * M1, 128:256])
        sz[2 * q, M1:] = jnp.where(left_h, t0, t1).astype(BF)
        sz[2 * q + 1, M1:] = jnp.where(left_h, t1, t0).astype(BF)
    for dc, dl in offs:
        cc, ll = lax.rem(c + dc, 4), lax.rem(l + dl, 2)
        send(sz.at[2 * cc + ll], fz.at[2 * c + l], S_GM + 2 * dc + dl, zdev(dc, dl))
    fz[2 * c + l] = sz[2 * c + l]

    for j in range(NJ):
        cols = pl.ds(j * NC, NC)
        for kind, dc in ((2, 1), (3, 3), (4, 1), (5, 3)):
            arrived(yrecv.at[kind, j], S_Y + 3 * kind + j, zdev(dc, 0))
        y_out[h0, cols] = (
            yp[yrow(c, 0), cols] + yrecv[4, j].astype(F32) + yrecv[3, j].astype(F32)
        ).astype(BF)
        y_out[h1, cols] = (
            yp[yrow(c, 1), cols] + yrecv[5, j].astype(F32) + yrecv[2, j].astype(F32)
        ).astype(BF)

    for i in (1, 3, 2):
        arrived(wrecv.at[i - 1], S_WS + i - 1, ydev(i))
    w_out[...] = (
        gw[k] + crecv[0].astype(F32)
        + wrecv[0].astype(F32) + wrecv[1].astype(F32) + wrecv[2].astype(F32)
    ).astype(BF)

    for dc, dl in offs:
        cc, ll = lax.rem(c + 4 - dc, 4), lax.rem(l + dl, 2)
        o = 2 * dc + dl
        arrived(fz.at[2 * cc + ll], S_GM + o, zdev(dc, dl))

    def unpack(lv):
        units = []
        for t in range(4):
            f = fz[2 * t].astype(F32) + fz[2 * t + 1].astype(F32)
            m, p = f[:M1], f[M1:]
            halves = [swap(p), p] if lv else [p, swap(p)]
            rem = (jnp.concatenate(halves, axis=0), jnp.concatenate(halves[::-1], axis=0))
            main = [(m, swap(m)), (swap(m), m)]
            units += [rem] + main if lv else main + [rem]
        for q in range(6):
            ga_out[:, 128 * q : 128 * q + 128] = jnp.where(
                left, units[2 * q][0], units[2 * q + 1][1]
            ).astype(BF)

    for lv in (0, 1):
        pl.when(l == lv)(lambda lv=lv: unpack(lv))

    for cp in pending:
        cp.wait_send()


def per_device(acts, w_out, grad_out):
    def vm(shape, dtype=BF):
        return pltpu.VMEM(shape, dtype)

    return pl.pallas_call(
        kernel,
        out_shape=[vm((M1, N)), vm((M1, 4 * KB)), vm((KB, N))],
        in_specs=[
            pl.BlockSpec(memory_space=pltpu.HBM),
            pl.BlockSpec(memory_space=pltpu.HBM),
            pl.BlockSpec(memory_space=pltpu.HBM),
        ],
        out_specs=[pl.BlockSpec(memory_space=pltpu.VMEM)] * 3,
        scratch_shapes=[
            vm((M1, 4 * KB)),
            vm((4, M1 + H, 128)),
            vm((4, MG, XB)),
            vm((8, M1 + H, 128)),
            vm((N, N)),
            vm((MG, N)),
            vm((4, XB, MG)),
            vm((MG, N), F32),
            vm((6, NJ, H, NC)),
            vm((6, NJ, H, NC)),
            vm((4, MG, XB)),
            vm((3, MG, XB)),
            vm((8, M1 + H, 128)),
            vm((8, M1 + H, 128)),
            vm((8, KB, N), F32),
            vm((4, KB, N)),
            vm((4, KB, N)),
            vm((3, KB, N)),
            vm((3, KB, N)),
            pltpu.SemaphoreType.DMA((N_SEM,)),
            pltpu.SemaphoreType.DMA((N_SEM,)),
            pltpu.SemaphoreType.DMA((4,)),
        ],
        compiler_params=pltpu.CompilerParams(
            collective_id=0, has_side_effects=True, vmem_limit_bytes=62 * 2**20
        ),
        cost_estimate=pl.CostEstimate(
            flops=6 * MG * N * N, bytes_accessed=3 * 2**20, transcendentals=0
        ),
    )(acts, w_out, grad_out)


def solution(mesh):
    spec = P(("depth", "col"), "row")
    return jax.shard_map(
        per_device, mesh=mesh, in_specs=(spec,) * 3, out_specs=(spec,) * 3, check_vma=False
    )
```
